256 devices in a mesh: layer: 4 (over y), feat: 32 (over z, x_hi, core), tok: 2 (over x_lo).
Axes of the slice: x: 4 (x_hi: 2, x_lo: 2; x = x_hi * 2 + x_lo), y: 4, z: 8, core: 2. Of those that a mesh axis runs over, the one named last changes fastest.
Arguments:
- resid: bfloat16 [4, 256, 3584], P('layer', 'tok'), may hold values from -6 to 6
- enc_weight: bfloat16 [4, 3584, 8192], P('layer', None, 'feat'), may hold values from -0.09375 to 0.09375
- enc_bias: float32 [4, 8192], P('layer', 'feat'), may hold values from -3 to 3
- active: int32 [4, 256, 8192], P('layer', 'tok', 'feat'), may hold values 0 or 1
- dec_weight: bfloat16 [4, 4, 8192, 3584], P('layer', None, 'feat', 'tok'), may hold values from -0.0625 to 0.0625
- target: bfloat16 [4, 256, 3584], P('layer', 'feat', 'tok'), may hold values from -6 to 6
Outputs:
- recon: bfloat16 [4, 256, 3584], P('layer', 'feat', 'tok')
- enc_grad: bfloat16 [4, 3584, 8192], P('layer', None, 'feat')
- bias_grad: float32 [4, 8192], P('layer', 'feat')
- dec_grad: bfloat16 [4, 4, 8192, 3584], P('layer', None, 'feat', 'tok')
The draws below stay inside these ranges and needn't reach their ends.
All inputs are finite; a program needn't handle non-finite values. No bound on the sum of `active` on one device may be relied on, other than what follows from the above.
Results may differ from the reference program's by a relative error of at most 0.0075.
Values may be sent and summed in bfloat16 or wider, within the bound.
No kernel may reach another device: no remote copies, remote signals or barrier semaphores. Data moves between devices by JAX's collectives and lax.ppermute only.
A program may use at most 128 MiB of HBM per device.

```python
import math
import jax
import jax.numpy as jnp
from jax import lax

D = 3584
F = 8192
LAYERS = 4
TOKENS = 256


def set_ends(values, key, smallest, top_value):
    index_at = [jax.random.randint(jax.random.fold_in(key, axis), (), 0, length) for axis, length in enumerate(values.shape)]
    longest = values.shape.index(max(values.shape))
    next_to = index_at[:longest] + [(index_at[longest] + 1) % values.shape[longest]] + index_at[longest + 1:]
    return values.at[tuple(index_at)].set(smallest).at[tuple(next_to)].set(top_value)


def levels(key, shape, cuts, smallest, high):
    def one(dim, parts):
        heights = jax.random.uniform(jax.random.fold_in(jax.random.fold_in(key, 6), dim), (parts,), jnp.float32, smallest / len(cuts), high / len(cuts))
        return jnp.repeat(jnp.exp(heights), shape[dim] // parts).reshape((-1,) + (1,) * (len(shape) - dim - 1))

    loudness = one(*cuts[0])
    for cut in cuts[1:]:
        loudness = loudness * one(*cut)
    return loudness


def centred(stream_key, dims, spread, reach, split=(), held_as=jnp.bfloat16):
    loudness = levels(stream_key, dims, split, -0.22, 0.18) if split else 1.0
    drawn = jax.random.normal(stream_key, dims, jnp.float32) * spread * loudness
    return jnp.minimum(jnp.maximum(drawn, -reach), reach).astype(held_as)


def setup_inputs(seed: int = 0) -> dict:
    arg_keys = jax.random.split(jax.random.key(seed), 7)
    return {
        "resid": centred(arg_keys[0], (LAYERS, TOKENS, D), 1.0, 6.0, ((0, 4), (1, 2))),
        "enc_weight": centred(arg_keys[1], (LAYERS, D, F), D ** -0.5, 0.09375, ((0, 4), (2, 32))),
        "enc_bias": centred(arg_keys[2], (LAYERS, F), 0.5, 3.0, ((0, 4), (1, 32)), jnp.float32),
        "active": set_ends((jax.random.randint(arg_keys[3], (LAYERS, TOKENS, F), 0, 4) < 1).astype(jnp.int32), jax.random.fold_in(arg_keys[3], 1), 0, 1),
        "dec_weight": centred(arg_keys[4], (LAYERS, LAYERS, F, D), F ** -0.5, 0.0625, ((0, 4), (2, 32), (3, 2))),
        "target": centred(arg_keys[5], (LAYERS, TOKENS, D), 1.0, 6.0, ((0, 4), (1, 32), (2, 2))),
    }


def contract_rows(left, right):
    return lax.dot_general(left, right, (((0,), (0,)), ((), ())), preferred_element_type=jnp.float32)

def contract_cols(left, right):
    return lax.dot_general(left, right, (((1,), (1,)), ((), ())), preferred_element_type=jnp.float32)

def reference(resid, enc_weight, enc_bias, active, dec_weight, target):
    layers = resid.shape[0]
    tokens_all = resid.shape[1]
    width = resid.shape[2]
    features = enc_weight.shape[2]
    inv_root = 1.0 / math.sqrt(tokens_all)
    codes = []
    for source in range(layers):
        preact = jnp.dot(resid[source], enc_weight[source], preferred_element_type=jnp.float32) + enc_bias[source][None, :]
        codes.append(jnp.where(active[source] == 1, preact, 0.0).astype(jnp.bfloat16))
    recon_list = []
    errors = []
    for target_pos in range(layers):
        decoded = jnp.zeros((tokens_all, width), jnp.float32)
        for source in range(target_pos + 1):
            decoded = decoded + jnp.dot(codes[source], dec_weight[source, target_pos], preferred_element_type=jnp.float32)
        recon_list.append(decoded.astype(jnp.bfloat16))
        errors.append(((decoded - target[target_pos].astype(jnp.float32)) * inv_root).astype(jnp.bfloat16))
    grad_rows = []
    enc_list = []
    bias_list = []
    for source in range(layers):
        row_blocks = []
        feat_grad = jnp.zeros((tokens_all, features), jnp.float32)
        for target_pos in range(layers):
            if target_pos >= source:
                row_blocks.append(contract_rows(codes[source], errors[target_pos]).astype(jnp.bfloat16))
                feat_grad = feat_grad + contract_cols(errors[target_pos], dec_weight[source, target_pos])
            else:
                row_blocks.append(jnp.zeros((features, width), jnp.bfloat16))
        grad_rows.append(jnp.stack(row_blocks))
        masked = jnp.where(active[source] == 1, feat_grad, 0.0)
        bias_list.append(lax.optimization_barrier(jnp.sum(masked, axis=0)))
        enc_list.append(contract_rows(resid[source], masked.astype(jnp.bfloat16)).astype(jnp.bfloat16))
    return (jnp.stack(recon_list), jnp.stack(enc_list), jnp.stack(bias_list), jnp.stack(grad_rows))
```

```python
import math

import jax
import jax.numpy as jnp
from jax import lax
from jax.sharding import Mesh, PartitionSpec as P

SWAP = [(0, 1), (1, 0)]
GROUP = ("z", "xh")
ROWS = 8


def batch_dot(left, right, left_dim, right_dim):
    return lax.dot_general(
        left,
        right,
        (((left_dim,), (right_dim,)), ((0,), (0,))),
        preferred_element_type=jnp.float32,
    )


def ordered(first, mine, other, axis):
    return jnp.where(
        first, jnp.concatenate([mine, other], axis), jnp.concatenate([other, mine], axis)
    )


def body(resid, enc_weight, enc_bias, active, dec_weight, target):
    layers, feat_shard, width = dec_weight.shape[1:]
    layer = lax.axis_index("y")
    core0 = lax.axis_index("core") == 0
    tok0 = lax.axis_index("tok") == 0
    resid_local = resid[0]
    weight = dec_weight[0]
    mask_local = active[0] == 1
    preact = (
        jnp.dot(resid_local, enc_weight[0], preferred_element_type=jnp.float32)
        + enc_bias[0][None, :]
    )
    codes_local = jnp.where(mask_local, preact, 0.0).astype(jnp.bfloat16)
    codes_other = lax.ppermute(codes_local, "tok", SWAP)
    codes = ordered(tok0, codes_local, codes_other, 0)
    tokens = codes.shape[0]
    groups = tokens // (2 * ROWS)
    half = tokens // 2
    inv_root = 1.0 / math.sqrt(tokens)

    resid_late, mask_late, codes = lax.optimization_barrier(
        (resid_local, mask_local.astype(jnp.bfloat16), codes)
    )
    resid_other = lax.ppermute(resid_late, "tok", SWAP)
    mask_other = lax.ppermute(mask_late, "tok", SWAP)

    by_core = codes.reshape(groups, 2, ROWS, feat_shard)
    codes_mine = jnp.where(core0, by_core[:, 0], by_core[:, 1]).reshape(half, feat_shard)
    codes_theirs = jnp.where(core0, by_core[:, 1], by_core[:, 0]).reshape(half, feat_shard)

    def decode(rows):
        rows = jnp.broadcast_to(rows[None], (layers,) + rows.shape)
        return batch_dot(rows, weight, 2, 1)

    sent = lax.ppermute(decode(codes_theirs).astype(jnp.bfloat16), "core", SWAP)
    pair = (decode(codes_mine) + sent.astype(jnp.float32)).astype(jnp.bfloat16)
    by_source = lax.all_to_all(pair, "y", 0, 0)
    used = (jnp.arange(layers) <= layer)[:, None, None]
    summed = jnp.sum(jnp.where(used, by_source.astype(jnp.float32), 0.0), axis=0)
    by_group = lax.all_to_all(
        summed.astype(jnp.bfloat16).reshape(groups, ROWS, width), GROUP, 0, 0
    )
    decoded = jnp.sum(by_group.astype(jnp.float32), axis=0)
    recon = decoded.astype(jnp.bfloat16)[None]
    error = ((decoded - target[0].astype(jnp.float32)) * inv_root).astype(jnp.bfloat16)

    own = lax.all_to_all(
        jnp.broadcast_to(error[None], (groups, ROWS, width)), GROUP, 0, 0
    ).reshape(half, width)
    wanted = (jnp.arange(layers) <= layer)[:, None, None]
    err_mine = lax.all_to_all(
        jnp.where(wanted, own[None], jnp.zeros((), own.dtype)), "y", 0, 0
    )
    err_theirs = lax.ppermute(err_mine, "core", SWAP)

    def back(err):
        return jnp.sum(batch_dot(err, weight, 2, 2), axis=0)

    fg_mine = back(err_mine).reshape(groups, 1, ROWS, feat_shard)
    fg_theirs = back(err_theirs).reshape(groups, 1, ROWS, feat_shard)
    feat_part = ordered(core0, fg_mine, fg_theirs, 1).reshape(tokens, feat_shard)
    feat_grad = feat_part + lax.ppermute(feat_part, "tok", SWAP)

    err_all = jnp.concatenate([err_mine, err_theirs], axis=1)
    codes_all = jnp.concatenate([codes_mine, codes_theirs], axis=0)
    codes_all = jnp.broadcast_to(codes_all[None], (layers,) + codes_all.shape)
    dec_grad = batch_dot(codes_all, err_all, 1, 1).astype(jnp.bfloat16)

    mask = ordered(tok0, mask_late, mask_other, 0)
    masked = jnp.where(mask > 0, feat_grad, 0.0)
    bias_grad = jnp.sum(masked, axis=0)
    resid_all = ordered(tok0, resid_late, resid_other, 0)
    enc_grad = lax.dot_general(
        resid_all,
        masked.astype(jnp.bfloat16),
        (((0,), (0,)), ((), ())),
        preferred_element_type=jnp.float32,
    ).astype(jnp.bfloat16)
    return recon, enc_grad[None], bias_grad[None], dec_grad[None]


def solution(mesh):
    layer, feat, tok = (mesh.shape[name] for name in ("layer", "feat", "tok"))
    fine = Mesh(
        mesh.devices.reshape(layer, feat // 4, 2, 2, tok), ("y", "z", "xh", "core", "tok")
    )
    feat_axes = ("z", "xh", "core")
    in_specs = (
        P("y", "tok", None),
        P("y", None, feat_axes),
        P("y", feat_axes),
        P("y", "tok", feat_axes),
        P("y", None, feat_axes, "tok"),
        P("y", feat_axes, "tok"),
    )
    out_specs = (
        P("y", feat_axes, "tok"),
        P("y", None, feat_axes),
        P("y", feat_axes),
        P("y", None, feat_axes, "tok"),
    )
    return jax.shard_map(body, mesh=fine, in_specs=in_specs, out_specs=out_specs, check_vma=False)
```

```python
import math

import jax
import jax.numpy as jnp
from jax import lax
from jax.sharding import Mesh, PartitionSpec as P

SWAP = [(0, 1), (1, 0)]
ROWS = 8


def batch_dot(left, right, left_dim, right_dim):
    return lax.dot_general(
        left,
        right,
        (((left_dim,), (right_dim,)), ((0,), (0,))),
        preferred_element_type=jnp.float32,
    )


def ordered(first, mine, other, axis):
    return jnp.where(
        first, jnp.concatenate([mine, other], axis), jnp.concatenate([other, mine], axis)
    )


def body(resid, enc_weight, enc_bias, active, dec_weight, target):
    layers, feat_shard, width = dec_weight.shape[1:]
    layer = lax.axis_index("y")
    core0 = lax.axis_index("core") == 0
    tok0 = lax.axis_index("tok") == 0
    resid_local = resid[0]
    weight = dec_weight[0]
    mask_local = active[0] == 1
    preact = (
        jnp.dot(resid_local, enc_weight[0], preferred_element_type=jnp.float32)
        + enc_bias[0][None, :]
    )
    codes_local = jnp.where(mask_local, preact, 0.0).astype(jnp.bfloat16)
    codes_other = lax.ppermute(codes_local, "tok", SWAP)
    codes = ordered(tok0, codes_local, codes_other, 0)
    tokens = codes.shape[0]
    zs = lax.axis_size("z")
    half = tokens // 2
    quarter = half // 2
    inv_root = 1.0 / math.sqrt(tokens)

    by_core = codes.reshape(zs, 2, 2, ROWS, feat_shard).transpose(2, 1, 0, 3, 4)
    codes_mine = jnp.where(core0, by_core[0], by_core[1]).reshape(half, feat_shard)
    codes_theirs = jnp.where(core0, by_core[1], by_core[0]).reshape(half, feat_shard)

    def decode(rows):
        rows = jnp.broadcast_to(rows[None], (layers,) + rows.shape)
        return batch_dot(rows, weight, 2, 1)

    sent = lax.ppermute(decode(codes_theirs).astype(jnp.bfloat16), "core", SWAP)
    pair = (decode(codes_mine) + sent.astype(jnp.float32)).astype(jnp.bfloat16)
    by_source = lax.all_to_all(
        pair.reshape(2 * layers, quarter, width), ("y", "xh"), 0, 0
    )
    used = (jnp.arange(2 * layers) // 2 <= layer)[:, None, None]
    summed = jnp.sum(jnp.where(used, by_source.astype(jnp.float32), 0.0), axis=0)
    summed = summed.astype(jnp.bfloat16).reshape(zs, ROWS, width)

    rows = resid_local.shape[0] // 2
    summed, resid_late = lax.optimization_barrier((summed, resid_local))
    fetch = jnp.where(core0, resid_late[:rows], resid_late[rows:])
    fetched = lax.ppermute(fetch, "tok", SWAP)
    by_group = lax.all_to_all(summed, "z", 0, 0)
    by_group, fetched = lax.optimization_barrier((by_group, fetched))
    decoded = jnp.sum(by_group.astype(jnp.float32), axis=0)
    recon = decoded.astype(jnp.bfloat16)[None]
    error = ((decoded - target[0].astype(jnp.float32)) * inv_root).astype(jnp.bfloat16)

    error, fetched, mask_late = lax.optimization_barrier(
        (error, fetched, mask_local.astype(jnp.bfloat16))
    )
    mask_other = lax.ppermute(mask_late, "tok", SWAP)
    fetched_other = lax.ppermute(fetched, "core", SWAP)
    own = lax.all_to_all(jnp.broadcast_to(error[None], (zs, ROWS, width)), "z", 0, 0)
    own, mask_other, fetched_other = lax.optimization_barrier((own, mask_other, fetched_other))
    resid_other = ordered(core0, fetched, fetched_other, 0)
    own = own.reshape(quarter, width)
    err_mine = lax.all_to_all(
        jnp.where(used, own[None], jnp.zeros((), own.dtype)), ("y", "xh"), 0, 0
    ).reshape(layers, half, width)
    err_theirs = lax.ppermute(err_mine, "core", SWAP)

    def back(err):
        return jnp.sum(batch_dot(err, weight, 2, 2), axis=0)

    fg_mine = back(err_mine).reshape(1, 2, zs, ROWS, feat_shard)
    fg_theirs = back(err_theirs).reshape(1, 2, zs, ROWS, feat_shard)
    feat_part = ordered(core0, fg_mine, fg_theirs, 0).transpose(2, 1, 0, 3, 4)
    feat_part = feat_part.reshape(tokens, feat_shard)
    feat_other = lax.ppermute(feat_part.astype(jnp.bfloat16), "tok", SWAP)
    feat_grad = feat_part + feat_other.astype(jnp.float32)

    err_all = jnp.concatenate([err_mine, err_theirs], axis=1)
    codes_all = jnp.concatenate([codes_mine, codes_theirs], axis=0)
    codes_all = jnp.broadcast_to(codes_all[None], (layers,) + codes_all.shape)
    dec_grad = batch_dot(codes_all, err_all, 1, 1).astype(jnp.bfloat16)

    mask = ordered(tok0, mask_late, mask_other, 0)
    masked = jnp.where(mask > 0, feat_grad, 0.0)
    bias_grad = jnp.sum(masked, axis=0)
    resid_all = ordered(tok0, resid_late, resid_other, 0)
    enc_grad = lax.dot_general(
        resid_all,
        masked.astype(jnp.bfloat16),
        (((0,), (0,)), ((), ())),
        preferred_element_type=jnp.float32,
    ).astype(jnp.bfloat16)
    return recon, enc_grad[None], bias_grad[None], dec_grad[None]


def solution(mesh):
    layer, feat, tok = (mesh.shape[name] for name in ("layer", "feat", "tok"))
    fine = Mesh(
        mesh.devices.reshape(layer, feat // 4, 2, 2, tok), ("y", "z", "xh", "core", "tok")
    )
    feat_axes = ("z", "xh", "core")
    in_specs = (
        P("y", "tok", None),
        P("y", None, feat_axes),
        P("y", feat_axes),
        P("y", "tok", feat_axes),
        P("y", None, feat_axes, "tok"),
        P("y", feat_axes, "tok"),
    )
    out_specs = (
        P("y", feat_axes, "tok"),
        P("y", None, feat_axes),
        P("y", feat_axes),
        P("y", None, feat_axes, "tok"),
    )
    return jax.shard_map(body, mesh=fine, in_specs=in_specs, out_specs=out_specs, check_vma=False)
```

```python
import math

import jax
import jax.numpy as jnp
from jax import lax
from jax.sharding import Mesh, PartitionSpec as P

SWAP = [(0, 1), (1, 0)]
ROWS = 8


def batch_dot(left, right, left_dim, right_dim):
    return lax.dot_general(
        left,
        right,
        (((left_dim,), (right_dim,)), ((0,), (0,))),
        preferred_element_type=jnp.float32,
    )


def ordered(first, mine, other, axis):
    return jnp.where(
        first, jnp.concatenate([mine, other], axis), jnp.concatenate([other, mine], axis)
    )


def body(resid, enc_weight, enc_bias, active, dec_weight, target):
    layers, feat_shard, width = dec_weight.shape[1:]
    layer = lax.axis_index("y")
    core0 = lax.axis_index("core") == 0
    tok0 = lax.axis_index("tok") == 0
    resid_local = resid[0]
    weight = dec_weight[0]
    mask_local = active[0] == 1
    preact = (
        jnp.dot(resid_local, enc_weight[0], preferred_element_type=jnp.float32)
        + enc_bias[0][None, :]
    )
    codes_local = jnp.where(mask_local, preact, 0.0).astype(jnp.bfloat16)
    codes_other = lax.ppermute(codes_local, "tok", SWAP)
    codes = ordered(tok0, codes_local, codes_other, 0)
    tokens = codes.shape[0]
    zs, peers = lax.axis_size("zh"), 2 * lax.axis_size("zh")
    half = tokens // 2
    quarter = half // 2
    inv_root = 1.0 / math.sqrt(tokens)

    by_core = codes.reshape(zs, 2, 2, 2, ROWS, feat_shard).transpose(3, 1, 0, 2, 4, 5)
    codes_mine = jnp.where(core0, by_core[0], by_core[1]).reshape(half, feat_shard)
    codes_theirs = jnp.where(core0, by_core[1], by_core[0]).reshape(half, feat_shard)

    def decode(rows, blocks):
        rows = jnp.broadcast_to(rows[None], (blocks.shape[0],) + rows.shape)
        return batch_dot(rows, blocks, 2, 1)

    sent = lax.ppermute(decode(codes_theirs, weight).astype(jnp.bfloat16), "core", SWAP)
    kept = lax.optimization_barrier(decode(codes_mine, weight))
    pair = (kept + sent.astype(jnp.float32)).astype(jnp.bfloat16)
    by_source = lax.all_to_all(
        pair.reshape(2 * layers, quarter, width), ("y", "zl"), 0, 0
    )
    used = (jnp.arange(2 * layers) // 2 <= layer)[:, None, None]
    summed = jnp.sum(jnp.where(used, by_source.astype(jnp.float32), 0.0), axis=0)
    summed = summed.astype(jnp.bfloat16).reshape(peers, ROWS, width)

    rows = resid_local.shape[0] // 2
    summed, resid_late, active_late = lax.optimization_barrier((summed, resid_local, active[0]))
    fetch = jnp.where(core0, resid_late[:rows], resid_late[rows:])
    fetched = lax.ppermute(fetch, "tok", SWAP)
    by_group = lax.all_to_all(summed, ("zh", "xh"), 0, 0)
    by_group, fetched = lax.optimization_barrier((by_group, fetched))
    decoded = jnp.sum(by_group.astype(jnp.float32), axis=0)
    recon = decoded.astype(jnp.bfloat16)[None]
    error = ((decoded - target[0].astype(jnp.float32)) * inv_root).astype(jnp.bfloat16)

    mask_late = (active_late == 1).astype(jnp.bfloat16)
    error, fetched, mask_late = lax.optimization_barrier((error, fetched, mask_late))
    mask_other = lax.ppermute(mask_late, "tok", SWAP)
    fetched_other = lax.ppermute(fetched, "core", SWAP)
    own = lax.all_to_all(
        jnp.broadcast_to(error[None], (peers, ROWS, width)), ("zh", "xh"), 0, 0
    )
    own, mask_other, fetched_other = lax.optimization_barrier((own, mask_other, fetched_other))
    resid_other = ordered(core0, fetched, fetched_other, 0)
    own = own.reshape(quarter, width)
    err_mine = lax.all_to_all(
        jnp.where(used, own[None], jnp.zeros((), own.dtype)), ("y", "zl"), 0, 0
    ).reshape(layers, half, width)
    err_theirs = lax.ppermute(err_mine, "core", SWAP)

    def back(err):
        return jnp.sum(batch_dot(err, weight, 2, 2), axis=0)

    fg_mine = back(err_mine).reshape(1, 2, zs, 2, ROWS, feat_shard)
    fg_theirs = back(err_theirs).reshape(1, 2, zs, 2, ROWS, feat_shard)
    feat_part = ordered(core0, fg_mine, fg_theirs, 0).transpose(2, 1, 3, 0, 4, 5)
    feat_part = feat_part.reshape(tokens, feat_shard)
    feat_other = lax.ppermute(feat_part.astype(jnp.bfloat16), "tok", SWAP)
    feat_grad = feat_part + feat_other.astype(jnp.float32)

    err_all = jnp.concatenate([err_mine, err_theirs], axis=1)
    codes_all = jnp.concatenate([codes_mine, codes_theirs], axis=0)
    codes_all = jnp.broadcast_to(codes_all[None], (layers,) + codes_all.shape)
    dec_grad = batch_dot(codes_all, err_all, 1, 1).astype(jnp.bfloat16)

    mask = ordered(tok0, mask_late, mask_other, 0)
    masked = jnp.where(mask > 0, feat_grad, 0.0)
    bias_grad = jnp.sum(masked, axis=0)
    resid_all = ordered(tok0, resid_late, resid_other, 0)
    enc_grad = lax.dot_general(
        resid_all,
        masked.astype(jnp.bfloat16),
        (((0,), (0,)), ((), ())),
        preferred_element_type=jnp.float32,
    ).astype(jnp.bfloat16)
    return recon, enc_grad[None], bias_grad[None], dec_grad[None]


def solution(mesh):
    layer, feat, tok = (mesh.shape[name] for name in ("layer", "feat", "tok"))
    fine = Mesh(
        mesh.devices.reshape(layer, feat // 8, 2, 2, 2, tok),
        ("y", "zh", "zl", "xh", "core", "tok"),
    )
    feat_axes = ("zh", "zl", "xh", "core")
    in_specs = (
        P("y", "tok", None),
        P("y", None, feat_axes),
        P("y", feat_axes),
        P("y", "tok", feat_axes),
        P("y", None, feat_axes, "tok"),
        P("y", feat_axes, "tok"),
    )
    out_specs = (
        P("y", feat_axes, "tok"),
        P("y", None, feat_axes),
        P("y", feat_axes),
        P("y", None, feat_axes, "tok"),
    )
    return jax.shard_map(body, mesh=fine, in_specs=in_specs, out_specs=out_specs, check_vma=False)
```

```python
import math

import jax
import jax.numpy as jnp
from jax import lax
from jax.sharding import Mesh, PartitionSpec as P

SWAP = [(0, 1), (1, 0)]
CROSS = [(0, 3), (1, 2), (2, 1), (3, 0)]
BOTH = ("core", "tok")
ROWS = 8


def batch_dot(left, right, left_dim, right_dim):
    dims = (((left_dim,), (right_dim,)), ((0,), (0,)))
    out = lax.dot_general(left, right, dims, preferred_element_type=jnp.float32)
    return lax.optimization_barrier(out)


def ordered(first, mine, other, axis):
    return jnp.where(
        first, jnp.concatenate([mine, other], axis), jnp.concatenate([other, mine], axis)
    )


def body(resid, enc_weight, enc_bias, active, dec_weight, target):
    layers, feat_shard, width = dec_weight.shape[1:]
    layer = lax.axis_index("y")
    core0 = lax.axis_index("core") == 0
    tok0 = lax.axis_index("tok") == 0
    zs, peers = lax.axis_size("zh"), 2 * lax.axis_size("zh")
    resid_local = resid[0]
    weight = dec_weight[0]
    weight_other = lax.ppermute(weight, "core", SWAP)
    preact = (
        jnp.dot(resid_local, enc_weight[0], preferred_element_type=jnp.float32)
        + enc_bias[0][None, :]
    )
    codes_local = jnp.where(active[0] == 1, preact, 0.0).astype(jnp.bfloat16)
    tokens = 2 * codes_local.shape[0]
    half, quarter = tokens // 2, tokens // 4
    inv_root = 1.0 / math.sqrt(tokens)

    split = codes_local.reshape(zs // 2, 2, 2, 2, ROWS, feat_shard).transpose(3, 1, 0, 2, 4, 5)
    local_mine = jnp.where(core0, split[0], split[1])
    local_theirs = jnp.where(core0, split[1], split[0])
    from_tok = lax.ppermute(jnp.stack([local_mine, local_theirs]), "tok", SWAP)
    from_core = lax.ppermute(local_theirs, "core", SWAP)
    from_cross = lax.ppermute(local_theirs, BOTH, CROSS)

    def whole(mine, other):
        return ordered(tok0, mine, other, 1).reshape(half, feat_shard)

    codes_mine = whole(local_mine, from_tok[0])
    codes_theirs = whole(local_theirs, from_tok[1])
    codes_other = whole(from_core, from_cross)
    targets = (jnp.arange(layers) >= layer)[:, None, None]

    def decode(rows, blocks):
        return batch_dot(jnp.where(targets, rows[None], jnp.zeros((), rows.dtype)), blocks, 2, 1)

    pair = (decode(codes_mine, weight) + decode(codes_other, weight_other)).astype(jnp.bfloat16)
    by_source = lax.all_to_all(
        pair.reshape(2 * layers, quarter, width), ("y", "zl"), 0, 0
    )
    summed = jnp.sum(by_source.astype(jnp.float32), axis=0)
    summed = summed.astype(jnp.bfloat16).reshape(peers, ROWS, width)

    rows = resid_local.shape[0] // 2
    summed, resid_late, active_late = lax.optimization_barrier((summed, resid_local, active[0]))
    fetch = jnp.where(core0, resid_late[:rows], resid_late[rows:])
    fetched = lax.ppermute(fetch, "tok", SWAP)
    by_group = lax.all_to_all(summed, ("zh", "xh"), 0, 0)
    by_group, fetched = lax.optimization_barrier((by_group, fetched))
    decoded = jnp.sum(by_group.astype(jnp.float32), axis=0)
    recon = decoded.astype(jnp.bfloat16)[None]
    error = ((decoded - target[0].astype(jnp.float32)) * inv_root).astype(jnp.bfloat16)

    mask_late = (active_late == 1).astype(jnp.bfloat16)
    error, fetched, mask_late = lax.optimization_barrier((error, fetched, mask_late))
    mask_other = lax.ppermute(mask_late, "tok", SWAP)
    fetched_other = lax.ppermute(fetched, "core", SWAP)
    own = lax.all_to_all(
        jnp.broadcast_to(error[None], (peers, ROWS, width)), ("zh", "xh"), 0, 0
    )
    own, mask_other, fetched_other = lax.optimization_barrier((own, mask_other, fetched_other))
    resid_other = ordered(core0, fetched, fetched_other, 0)
    own = own.reshape(quarter, width)
    wanted = (jnp.arange(2 * layers) // 2 <= layer)[:, None, None]
    err_mine = lax.all_to_all(
        jnp.where(wanted, own[None], jnp.zeros((), own.dtype)), ("y", "zl"), 0, 0
    ).reshape(layers, half, width)
    err_theirs = lax.ppermute(err_mine, "core", SWAP)

    def back(blocks):
        return jnp.sum(batch_dot(err_mine, blocks, 2, 2), axis=0)

    feat_mine = back(weight)
    feat_other = back(weight_other).astype(jnp.bfloat16)
    got_tok = lax.ppermute(feat_mine.astype(jnp.bfloat16), "tok", SWAP)
    got_core = lax.ppermute(feat_other, "core", SWAP)
    got_cross = lax.ppermute(feat_other, BOTH, CROSS)

    err_all = jnp.concatenate([err_mine, err_theirs], axis=1)
    codes_all = jnp.concatenate([codes_mine, codes_theirs], axis=0)
    codes_all = jnp.broadcast_to(codes_all[None], (layers,) + codes_all.shape)
    dec_grad = batch_dot(codes_all, err_all, 1, 1).astype(jnp.bfloat16)

    got_tok, got_core, got_cross, dec_grad = lax.optimization_barrier(
        (got_tok, got_core, got_cross, dec_grad)
    )
    grad_mine = feat_mine + got_tok.astype(jnp.float32)
    grad_theirs = got_core.astype(jnp.float32) + got_cross.astype(jnp.float32)
    feat_grad = ordered(core0, grad_mine[None], grad_theirs[None], 0)
    feat_grad = feat_grad.reshape(2, 2, zs, 2, ROWS, feat_shard).transpose(2, 1, 3, 0, 4, 5)
    feat_grad = feat_grad.reshape(tokens, feat_shard)
    mask = ordered(tok0, mask_late, mask_other, 0)
    masked = jnp.where(mask > 0, feat_grad, 0.0)
    bias_grad = jnp.sum(masked, axis=0)
    resid_all = ordered(tok0, resid_late, resid_other, 0)
    enc_grad = lax.dot_general(
        resid_all,
        masked.astype(jnp.bfloat16),
        (((0,), (0,)), ((), ())),
        preferred_element_type=jnp.float32,
    ).astype(jnp.bfloat16)
    return recon, enc_grad[None], bias_grad[None], dec_grad[None]


def solution(mesh):
    layer, feat, tok = (mesh.shape[name] for name in ("layer", "feat", "tok"))
    fine = Mesh(
        mesh.devices.reshape(layer, feat // 8, 2, 2, 2, tok),
        ("y", "zh", "zl", "xh", "core", "tok"),
    )
    feat_axes = ("zh", "zl", "xh", "core")
    in_specs = (
        P("y", "tok", None),
        P("y", None, feat_axes),
        P("y", feat_axes),
        P("y", "tok", feat_axes),
        P("y", None, feat_axes, "tok"),
        P("y", feat_axes, "tok"),
    )
    out_specs = (
        P("y", feat_axes, "tok"),
        P("y", None, feat_axes),
        P("y", feat_axes),
        P("y", None, feat_axes, "tok"),
    )
    return jax.shard_map(body, mesh=fine, in_specs=in_specs, out_specs=out_specs, check_vma=False)
```

```python
import math

import jax
import jax.numpy as jnp
from jax import lax
from jax.experimental import pallas as pl
from jax.experimental.pallas import tpu as pltpu
from jax.sharding import Mesh, PartitionSpec as P

SWAP = [(0, 1), (1, 0)]
CROSS = [(0, 3), (1, 2), (2, 1), (3, 0)]
BOTH = ("core", "tok")
ROWS = 8


PARAMS = pltpu.CompilerParams(vmem_limit_bytes=20 * 1024 * 1024)


def cost(flops, *arrays):
    moved = sum(a.size * a.dtype.itemsize for a in arrays)
    return pl.CostEstimate(flops=flops, bytes_accessed=moved, transcendentals=0)


def product(left, right, left_dim, right_dim):
    dims = (((left_dim,), (right_dim,)), ((), ()))
    return lax.dot_general(left, right, dims, preferred_element_type=jnp.float32)


def decode_kernel(layer_ref, mine_ref, other_ref, weight_ref, weight_other_ref, out_ref):
    used = pl.program_id(0) >= layer_ref[0]

    @pl.when(used)
    def _():
        total = product(mine_ref[...], weight_ref[0], 1, 0)
        total = total + product(other_ref[...], weight_other_ref[0], 1, 0)
        out_ref[0] = total.astype(out_ref.dtype)

    @pl.when(jnp.logical_not(used))
    def _():
        out_ref[...] = jnp.zeros_like(out_ref)


def decode(layer, mine, other, weight, weight_other):
    layers, feat_shard, width = weight.shape
    rows = mine.shape[0]
    small = pl.BlockSpec((rows, feat_shard), lambda m, _: (0, 0))
    large = pl.BlockSpec((1, feat_shard, width), lambda m, _: (m, 0, 0))
    out = jax.ShapeDtypeStruct((layers, rows, width), jnp.bfloat16)
    return pl.pallas_call(
        decode_kernel,
        out_shape=out,
        grid_spec=pltpu.PrefetchScalarGridSpec(
            num_scalar_prefetch=1,
            grid=(layers,),
            in_specs=[small, small, large, large],
            out_specs=pl.BlockSpec((1, rows, width), lambda m, _: (m, 0, 0)),
        ),
        compiler_params=PARAMS,
        cost_estimate=cost(4 * rows * weight.size, weight, weight_other, out),
    )(layer.reshape(1), mine, other, weight, weight_other)


def back_kernel(err_ref, weight_ref, weight_other_ref, mine_ref, sent_ref, other_ref, total):
    step = pl.program_id(0)
    mine = product(err_ref[0], weight_ref[0], 1, 1)
    other = product(err_ref[0], weight_other_ref[0], 1, 1)

    @pl.when(step == 0)
    def _():
        mine_ref[...] = mine
        total[...] = other

    @pl.when(step > 0)
    def _():
        mine_ref[...] += mine
        total[...] += other

    @pl.when(step == pl.num_programs(0) - 1)
    def _():
        sent_ref[...] = mine_ref[...].astype(sent_ref.dtype)
        other_ref[...] = total[...].astype(other_ref.dtype)


def back(err, weight, weight_other):
    layers, feat_shard, width = weight.shape
    rows = err.shape[1]
    small = pl.BlockSpec((rows, feat_shard), lambda m: (0, 0))
    large = pl.BlockSpec((1, feat_shard, width), lambda m: (m, 0, 0))
    half = jax.ShapeDtypeStruct((rows, feat_shard), jnp.bfloat16)
    return pl.pallas_call(
        back_kernel,
        out_shape=[jax.ShapeDtypeStruct((rows, feat_shard), jnp.float32), half, half],
        grid=(layers,),
        in_specs=[pl.BlockSpec((1, rows, width), lambda m: (m, 0, 0)), large, large],
        out_specs=[small, small, small],
        scratch_shapes=[pltpu.VMEM((rows, feat_shard), jnp.float32)],
        compiler_params=PARAMS,
        cost_estimate=cost(4 * rows * weight.size, weight, weight_other, err),
    )(err, weight, weight_other)


def grad_kernel(codes_ref, mine_ref, theirs_ref, out_ref):
    half = mine_ref.shape[1]
    total = product(codes_ref[:, :half], mine_ref[0], 1, 0)
    total = total + product(codes_ref[:, half:], theirs_ref[0], 1, 0)
    out_ref[0] = total.astype(out_ref.dtype)


def decoder_grad(codes, mine, theirs):
    layers, half, width = mine.shape
    feat_shard = codes.shape[0]
    err = pl.BlockSpec((1, half, width), lambda m: (m, 0, 0))
    out = jax.ShapeDtypeStruct((layers, feat_shard, width), jnp.bfloat16)
    return pl.pallas_call(
        grad_kernel,
        out_shape=out,
        grid=(layers,),
        in_specs=[pl.BlockSpec(codes.shape, lambda m: (0, 0)), err, err],
        out_specs=pl.BlockSpec((1, feat_shard, width), lambda m: (m, 0, 0)),
        compiler_params=PARAMS,
        cost_estimate=cost(4 * feat_shard * mine.size, mine, theirs, out),
    )(codes, mine, theirs)


def sum_kernel(parts_ref, out_ref):
    total = parts_ref[0].astype(jnp.float32)
    for part in range(1, parts_ref.shape[0]):
        total = total + parts_ref[part].astype(jnp.float32)
    out_ref[...] = total.astype(out_ref.dtype)


def sum_parts(parts, pieces=2):
    count, rows, width = parts.shape
    out = jax.ShapeDtypeStruct((rows, width), jnp.bfloat16)
    return pl.pallas_call(
        sum_kernel,
        out_shape=out,
        grid=(pieces,),
        in_specs=[pl.BlockSpec((count, rows // pieces, width), lambda i: (0, i, 0))],
        out_specs=pl.BlockSpec((rows // pieces, width), lambda i: (i, 0)),
        compiler_params=PARAMS,
        cost_estimate=cost(parts.size, parts, out),
    )(parts)


def ordered(first, mine, other, axis):
    return jnp.where(
        first, jnp.concatenate([mine, other], axis), jnp.concatenate([other, mine], axis)
    )


def body(resid, enc_weight, enc_bias, active, dec_weight, target):
    layers, feat_shard, width = dec_weight.shape[1:]
    layer = lax.axis_index("y")
    core0 = lax.axis_index("core") == 0
    tok0 = lax.axis_index("tok") == 0
    zs, peers = lax.axis_size("zh"), 2 * lax.axis_size("zh")
    resid_local = resid[0]
    weight = dec_weight[0]
    weight_other = lax.ppermute(weight, "core", SWAP)
    preact = (
        jnp.dot(resid_local, enc_weight[0], preferred_element_type=jnp.float32)
        + enc_bias[0][None, :]
    )
    codes_local = jnp.where(active[0] == 1, preact, 0.0).astype(jnp.bfloat16)
    tokens = 2 * codes_local.shape[0]
    half, quarter = tokens // 2, tokens // 4
    inv_root = 1.0 / math.sqrt(tokens)

    split = codes_local.reshape(zs // 2, 2, 2, 2, ROWS, feat_shard).transpose(3, 1, 0, 2, 4, 5)
    local_mine = jnp.where(core0, split[0], split[1])
    local_theirs = jnp.where(core0, split[1], split[0])
    from_tok = lax.ppermute(jnp.stack([local_mine, local_theirs]), "tok", SWAP)
    from_core = lax.ppermute(local_theirs, "core", SWAP)
    from_cross = lax.ppermute(local_theirs, BOTH, CROSS)

    def whole(mine, other):
        return ordered(tok0, mine, other, 1).reshape(half, feat_shard)

    codes_mine = whole(local_mine, from_tok[0])
    codes_theirs = whole(local_theirs, from_tok[1])
    codes_other = whole(from_core, from_cross)

    rows = resid_local.shape[0] // 2
    codes_mine, resid_late, active_late = lax.optimization_barrier(
        (codes_mine, resid_local, active[0])
    )
    mask_late = (active_late == 1).astype(jnp.bfloat16)
    fetched = lax.ppermute(jnp.where(core0, resid_late[:rows], resid_late[rows:]), "tok", SWAP)
    mask_other = lax.ppermute(mask_late, "tok", SWAP)
    pair = decode(layer, codes_mine, codes_other, weight, weight_other)
    by_source = lax.all_to_all(
        pair.reshape(2 * layers, quarter, width), ("y", "zl"), 0, 0
    )
    by_source, fetched, mask_other = lax.optimization_barrier((by_source, fetched, mask_other))
    fetched_other = lax.ppermute(fetched, "core", SWAP)
    summed = sum_parts(by_source).reshape(peers, ROWS, width)
    by_group = lax.all_to_all(summed, ("zh", "xh"), 0, 0)
    by_group, fetched_other = lax.optimization_barrier((by_group, fetched_other))
    decoded = jnp.sum(by_group.astype(jnp.float32), axis=0)
    recon = decoded.astype(jnp.bfloat16)[None]
    error = ((decoded - target[0].astype(jnp.float32)) * inv_root).astype(jnp.bfloat16)

    own = lax.all_to_all(
        jnp.broadcast_to(error[None], (peers, ROWS, width)), ("zh", "xh"), 0, 0
    )
    own = own.reshape(quarter, width)
    wanted = (jnp.arange(2 * layers) // 2 <= layer)[:, None, None]
    err_mine = lax.all_to_all(
        jnp.where(wanted, own[None], jnp.zeros((), own.dtype)), ("y", "zl"), 0, 0
    ).reshape(layers, half, width)
    err_theirs = lax.ppermute(err_mine, "core", SWAP)

    feat_mine, feat_sent, feat_other = back(err_mine, weight, weight_other)
    got_tok = lax.ppermute(feat_sent, "tok", SWAP)
    got_cross = lax.ppermute(feat_other, BOTH, CROSS)
    got_core = lax.ppermute(feat_other, "core", SWAP)

    feat_mine, resid_late, fetched, fetched_other, mask_late, mask_other = lax.optimization_barrier(
        (feat_mine, resid_late, fetched, fetched_other, mask_late, mask_other)
    )
    feat_mine, codes_mine, codes_theirs = lax.optimization_barrier(
        (feat_mine, codes_mine, codes_theirs)
    )
    resid_other = ordered(core0, fetched, fetched_other, 0)
    codes_all = jnp.concatenate([codes_mine, codes_theirs], axis=0).T
    dec_grad = decoder_grad(codes_all, err_mine, err_theirs)
    got_tok, got_core, got_cross, dec_grad = lax.optimization_barrier(
        (got_tok, got_core, got_cross, dec_grad)
    )
    grad_mine = feat_mine + got_tok.astype(jnp.float32)
    grad_theirs = got_core.astype(jnp.float32) + got_cross.astype(jnp.float32)
    feat_grad = ordered(core0, grad_mine[None], grad_theirs[None], 0)
    feat_grad = feat_grad.reshape(2, 2, zs, 2, ROWS, feat_shard).transpose(2, 1, 3, 0, 4, 5)
    feat_grad = feat_grad.reshape(tokens, feat_shard)
    mask = ordered(tok0, mask_late, mask_other, 0)
    masked = jnp.where(mask > 0, feat_grad, 0.0)
    bias_grad = jnp.sum(masked, axis=0)
    resid_all = ordered(tok0, resid_late, resid_other, 0)
    enc_grad = lax.dot_general(
        resid_all,
        masked.astype(jnp.bfloat16),
        (((0,), (0,)), ((), ())),
        preferred_element_type=jnp.float32,
    ).astype(jnp.bfloat16)
    return recon, enc_grad[None], bias_grad[None], dec_grad[None]


def solution(mesh):
    layer, feat, tok = (mesh.shape[name] for name in ("layer", "feat", "tok"))
    fine = Mesh(
        mesh.devices.reshape(layer, feat // 8, 2, 2, 2, tok),
        ("y", "zh", "zl", "xh", "core", "tok"),
    )
    feat_axes = ("zh", "zl", "xh", "core")
    in_specs = (
        P("y", "tok", None),
        P("y", None, feat_axes),
        P("y", feat_axes),
        P("y", "tok", feat_axes),
        P("y", None, feat_axes, "tok"),
        P("y", feat_axes, "tok"),
    )
    out_specs = (
        P("y", feat_axes, "tok"),
        P("y", None, feat_axes),
        P("y", feat_axes),
        P("y", None, feat_axes, "tok"),
    )
    return jax.shard_map(body, mesh=fine, in_specs=in_specs, out_specs=out_specs, check_vma=False)
```

```python
import math

import jax
import jax.numpy as jnp
from jax import lax
from jax.experimental import pallas as pl
from jax.experimental.pallas import tpu as pltpu
from jax.sharding import Mesh, PartitionSpec as P

SWAP = [(0, 1), (1, 0)]
CROSS = [(0, 3), (1, 2), (2, 1), (3, 0)]
BOTH = ("core", "tok")
ROWS = 8


PARAMS = pltpu.CompilerParams(vmem_limit_bytes=20 * 1024 * 1024)


def cost(flops, *arrays):
    moved = sum(a.size * a.dtype.itemsize for a in arrays)
    return pl.CostEstimate(flops=flops, bytes_accessed=moved, transcendentals=0)


def product(left, right, left_dim, right_dim):
    dims = (((left_dim,), (right_dim,)), ((), ()))
    return lax.dot_general(left, right, dims, preferred_element_type=jnp.float32)


def decode_kernel(layer_ref, mine_ref, other_ref, weight_ref, weight_other_ref, out_ref):
    used = pl.program_id(0) >= layer_ref[0]

    @pl.when(used)
    def _():
        total = product(mine_ref[...], weight_ref[0], 1, 0)
        total = total + product(other_ref[...], weight_other_ref[0], 1, 0)
        out_ref[0] = total.astype(out_ref.dtype)

    @pl.when(jnp.logical_not(used))
    def _():
        out_ref[...] = jnp.zeros_like(out_ref)


def decode(layer, mine, other, weight, weight_other):
    layers, feat_shard, width = weight.shape
    rows = mine.shape[0]
    small = pl.BlockSpec((rows, feat_shard), lambda m, _: (0, 0))
    large = pl.BlockSpec((1, feat_shard, width), lambda m, _: (m, 0, 0))
    out = jax.ShapeDtypeStruct((layers, rows, width), jnp.bfloat16)
    return pl.pallas_call(
        decode_kernel,
        out_shape=out,
        grid_spec=pltpu.PrefetchScalarGridSpec(
            num_scalar_prefetch=1,
            grid=(layers,),
            in_specs=[small, small, large, large],
            out_specs=pl.BlockSpec((1, rows, width), lambda m, _: (m, 0, 0)),
        ),
        compiler_params=PARAMS,
        cost_estimate=cost(4 * rows * weight.size, weight, weight_other, out),
    )(layer.reshape(1), mine, other, weight, weight_other)


def back_kernel(
    err_ref, weight_ref, weight_other_ref, mine_ref, sent_ref, other_ref, total_mine, total
):
    step = pl.program_id(0)
    err = err_ref[0].T
    mine = product(weight_ref[0], err, 1, 0)
    other = product(weight_other_ref[0], err, 1, 0)

    @pl.when(step == 0)
    def _():
        total_mine[...] = mine
        total[...] = other

    @pl.when(step > 0)
    def _():
        total_mine[...] += mine
        total[...] += other

    @pl.when(step == pl.num_programs(0) - 1)
    def _():
        whole = total_mine[...].T
        mine_ref[...] = whole
        sent_ref[...] = whole.astype(sent_ref.dtype)
        other_ref[...] = total[...].T.astype(other_ref.dtype)


def back(err, weight, weight_other):
    layers, feat_shard, width = weight.shape
    rows = err.shape[1]
    small = pl.BlockSpec((rows, feat_shard), lambda m: (0, 0))
    large = pl.BlockSpec((1, feat_shard, width), lambda m: (m, 0, 0))
    half = jax.ShapeDtypeStruct((rows, feat_shard), jnp.bfloat16)
    return pl.pallas_call(
        back_kernel,
        out_shape=[jax.ShapeDtypeStruct((rows, feat_shard), jnp.float32), half, half],
        grid=(layers,),
        in_specs=[pl.BlockSpec((1, rows, width), lambda m: (m, 0, 0)), large, large],
        out_specs=[small, small, small],
        scratch_shapes=[pltpu.VMEM((feat_shard, rows), jnp.float32)] * 2,
        compiler_params=PARAMS,
        cost_estimate=cost(4 * rows * weight.size, weight, weight_other, err),
    )(err, weight, weight_other)


def grad_kernel(codes_ref, mine_ref, theirs_ref, out_ref):
    err = jnp.concatenate([mine_ref[0], theirs_ref[0]], axis=0)
    total = product(codes_ref[...], err, 1, 0)
    out_ref[0] = total.astype(out_ref.dtype)


def decoder_grad(codes, mine, theirs):
    layers, half, width = mine.shape
    feat_shard = codes.shape[0]
    err = pl.BlockSpec((1, half, width), lambda m: (m, 0, 0))
    out = jax.ShapeDtypeStruct((layers, feat_shard, width), jnp.bfloat16)
    return pl.pallas_call(
        grad_kernel,
        out_shape=out,
        grid=(layers,),
        in_specs=[pl.BlockSpec(codes.shape, lambda m: (0, 0)), err, err],
        out_specs=pl.BlockSpec((1, feat_shard, width), lambda m: (m, 0, 0)),
        compiler_params=PARAMS,
        cost_estimate=cost(4 * feat_shard * mine.size, mine, theirs, out),
    )(codes, mine, theirs)


def sum_kernel(parts_ref, out_ref):
    total = parts_ref[0].astype(jnp.float32)
    for part in range(1, parts_ref.shape[0]):
        total = total + parts_ref[part].astype(jnp.float32)
    out_ref[...] = total.astype(out_ref.dtype)


def sum_parts(parts, pieces=2):
    count, rows, width = parts.shape
    out = jax.ShapeDtypeStruct((rows, width), jnp.bfloat16)
    return pl.pallas_call(
        sum_kernel,
        out_shape=out,
        grid=(pieces,),
        in_specs=[pl.BlockSpec((count, rows // pieces, width), lambda i: (0, i, 0))],
        out_specs=pl.BlockSpec((rows // pieces, width), lambda i: (i, 0)),
        compiler_params=PARAMS,
        cost_estimate=cost(parts.size, parts, out),
    )(parts)


def ordered(first, mine, other, axis):
    return jnp.where(
        first, jnp.concatenate([mine, other], axis), jnp.concatenate([other, mine], axis)
    )


def body(resid, enc_weight, enc_bias, active, dec_weight, target):
    layers, feat_shard, width = dec_weight.shape[1:]
    layer = lax.axis_index("y")
    core0 = lax.axis_index("core") == 0
    tok0 = lax.axis_index("tok") == 0
    zs, peers = lax.axis_size("zh"), 2 * lax.axis_size("zh")
    resid_local = resid[0]
    weight = dec_weight[0]
    weight_other = lax.ppermute(weight, "core", SWAP)
    preact = (
        jnp.dot(resid_local, enc_weight[0], preferred_element_type=jnp.float32)
        + enc_bias[0][None, :]
    )
    codes_local = jnp.where(active[0] == 1, preact, 0.0).astype(jnp.bfloat16)
    tokens = 2 * codes_local.shape[0]
    half, quarter = tokens // 2, tokens // 4
    inv_root = 1.0 / math.sqrt(tokens)

    split = codes_local.reshape(zs // 2, 2, 2, 2, ROWS, feat_shard).transpose(3, 1, 0, 2, 4, 5)
    local_mine = jnp.where(core0, split[0], split[1])
    local_theirs = jnp.where(core0, split[1], split[0])
    from_tok = lax.ppermute(jnp.stack([local_mine, local_theirs]), "tok", SWAP)
    from_core = lax.ppermute(local_theirs, "core", SWAP)
    from_cross = lax.ppermute(local_theirs, BOTH, CROSS)

    def whole(mine, other):
        return ordered(tok0, mine, other, 1).reshape(half, feat_shard)

    codes_mine = whole(local_mine, from_tok[0])
    codes_theirs = whole(local_theirs, from_tok[1])
    codes_other = whole(from_core, from_cross)

    rows = resid_local.shape[0] // 2
    mask_late = (active[0] == 1).astype(jnp.bfloat16)
    fetch = jnp.where(core0, resid_local[:rows], resid_local[rows:])
    codes_mine, fetch, mask_late = lax.optimization_barrier((codes_mine, fetch, mask_late))
    fetched = lax.ppermute(fetch, "tok", SWAP)
    mask_other = lax.ppermute(mask_late, "tok", SWAP)
    pair = decode(layer, codes_mine, codes_other, weight, weight_other)
    by_source = lax.all_to_all(
        pair.reshape(2 * layers, quarter, width), ("y", "zl"), 0, 0
    )
    by_source, fetched, mask_other = lax.optimization_barrier((by_source, fetched, mask_other))
    fetched_other = lax.ppermute(fetched, "core", SWAP)
    summed = sum_parts(by_source).reshape(peers, ROWS, width)
    by_group = lax.all_to_all(summed, ("zh", "xh"), 0, 0)
    by_group, fetched_other = lax.optimization_barrier((by_group, fetched_other))
    decoded = jnp.sum(by_group.astype(jnp.float32), axis=0)
    error = ((decoded - target[0].astype(jnp.float32)) * inv_root).astype(jnp.bfloat16)

    own = lax.all_to_all(
        jnp.broadcast_to(error[None], (peers, ROWS, width)), ("zh", "xh"), 0, 0
    )
    own, fetched, fetched_other, mask_late, mask_other, codes_mine, codes_theirs, decoded = (
        lax.optimization_barrier(
            (own, fetched, fetched_other, mask_late, mask_other, codes_mine, codes_theirs, decoded)
        )
    )
    own = own.reshape(quarter, width)
    wanted = (jnp.arange(2 * layers) // 2 <= layer)[:, None, None]
    spread = jnp.where(wanted, own[None], jnp.zeros((), own.dtype))
    err_mine = lax.all_to_all(spread, ("y", "zl"), 0, 0).reshape(layers, half, width)
    resid_other = ordered(core0, fetched, fetched_other, 0)
    resid_all = ordered(tok0, resid_local, resid_other, 0)
    mask = ordered(tok0, mask_late, mask_other, 0)
    codes_all = jnp.concatenate([codes_mine, codes_theirs], axis=0).T
    recon = decoded.astype(jnp.bfloat16)[None]
    err_mine, resid_all, mask, codes_all, recon = lax.optimization_barrier(
        (err_mine, resid_all, mask, codes_all, recon)
    )
    err_theirs = lax.ppermute(err_mine, "core", SWAP)

    feat_mine, feat_sent, feat_other = back(err_mine, weight, weight_other)
    got_tok = lax.ppermute(feat_sent, "tok", SWAP)
    got_cross = lax.ppermute(feat_other, BOTH, CROSS)
    got_core = lax.ppermute(feat_other, "core", SWAP)

    dec_grad = decoder_grad(codes_all, err_mine, err_theirs)
    got_tok, got_core, got_cross, dec_grad = lax.optimization_barrier(
        (got_tok, got_core, got_cross, dec_grad)
    )
    grad_mine = feat_mine + got_tok.astype(jnp.float32)
    grad_theirs = got_core.astype(jnp.float32) + got_cross.astype(jnp.float32)
    feat_grad = ordered(core0, grad_mine[None], grad_theirs[None], 0)
    feat_grad = feat_grad.reshape(2, 2, zs, 2, ROWS, feat_shard).transpose(2, 1, 3, 0, 4, 5)
    feat_grad = feat_grad.reshape(tokens, feat_shard)
    masked = jnp.where(mask > 0, feat_grad, 0.0)
    bias_grad = jnp.sum(masked, axis=0)
    enc_grad = lax.dot_general(
        resid_all,
        masked.astype(jnp.bfloat16),
        (((0,), (0,)), ((), ())),
        preferred_element_type=jnp.float32,
    ).astype(jnp.bfloat16)
    return recon, enc_grad[None], bias_grad[None], dec_grad[None]


def solution(mesh):
    layer, feat, tok = (mesh.shape[name] for name in ("layer", "feat", "tok"))
    fine = Mesh(
        mesh.devices.reshape(layer, feat // 8, 2, 2, 2, tok),
        ("y", "zh", "zl", "xh", "core", "tok"),
    )
    feat_axes = ("zh", "zl", "xh", "core")
    in_specs = (
        P("y", "tok", None),
        P("y", None, feat_axes),
        P("y", feat_axes),
        P("y", "tok", feat_axes),
        P("y", None, feat_axes, "tok"),
        P("y", feat_axes, "tok"),
    )
    out_specs = (
        P("y", feat_axes, "tok"),
        P("y", None, feat_axes),
        P("y", feat_axes),
        P("y", None, feat_axes, "tok"),
    )
    return jax.shard_map(body, mesh=fine, in_specs=in_specs, out_specs=out_specs, check_vma=False)
```

```python
import math

import jax
import jax.numpy as jnp
from jax import lax
from jax.experimental import pallas as pl
from jax.experimental.pallas import tpu as pltpu
from jax.sharding import Mesh, PartitionSpec as P

SWAP = [(0, 1), (1, 0)]
CROSS = [(0, 3), (1, 2), (2, 1), (3, 0)]
BOTH = ("core", "tok")
ROWS = 8


PARAMS = pltpu.CompilerParams(vmem_limit_bytes=12 * 1024 * 1024)


def cost(flops, *arrays):
    moved = sum(a.size * a.dtype.itemsize for a in arrays)
    return pl.CostEstimate(flops=flops, bytes_accessed=moved, transcendentals=0)


def product(left, right, left_dim, right_dim):
    dims = (((left_dim,), (right_dim,)), ((), ()))
    return lax.dot_general(left, right, dims, preferred_element_type=jnp.float32)


def decode_kernel(layer_ref, mine_ref, other_ref, weight_ref, weight_other_ref, out_ref):
    used = pl.program_id(0) >= layer_ref[0]

    @pl.when(used)
    def _():
        total = product(mine_ref[...], weight_ref[0], 1, 0)
        total = total + product(other_ref[...], weight_other_ref[0], 1, 0)
        out_ref[0] = total.astype(out_ref.dtype)

    @pl.when(jnp.logical_not(used))
    def _():
        out_ref[...] = jnp.zeros_like(out_ref)


def decode(layer, mine, other, weight, weight_other):
    layers, feat_shard, width = weight.shape
    rows = mine.shape[0]
    small = pl.BlockSpec((rows, feat_shard), lambda m, _: (0, 0))
    large = pl.BlockSpec((1, feat_shard, width), lambda m, _: (m, 0, 0))
    out = jax.ShapeDtypeStruct((layers, rows, width), jnp.bfloat16)
    return pl.pallas_call(
        decode_kernel,
        out_shape=pltpu.HBM(out.shape, out.dtype),
        grid_spec=pltpu.PrefetchScalarGridSpec(
            num_scalar_prefetch=1,
            grid=(layers,),
            in_specs=[small, small, large, large],
            out_specs=pl.BlockSpec((1, rows, width), lambda m, _: (m, 0, 0)),
        ),
        compiler_params=PARAMS,
        cost_estimate=cost(4 * rows * weight.size, weight, weight_other, out),
    )(layer.reshape(1), mine, other, weight, weight_other)


def back_kernel(
    err_ref, weight_ref, weight_other_ref, mine_ref, sent_ref, other_ref, total_mine, total
):
    step = pl.program_id(0)
    err = err_ref[0].T
    mine = product(weight_ref[0], err, 1, 0)
    other = product(weight_other_ref[0], err, 1, 0)

    @pl.when(step == 0)
    def _():
        total_mine[...] = mine
        total[...] = other

    @pl.when(step > 0)
    def _():
        total_mine[...] += mine
        total[...] += other

    @pl.when(step == pl.num_programs(0) - 1)
    def _():
        whole = total_mine[...].T
        mine_ref[...] = whole
        sent_ref[...] = whole.astype(sent_ref.dtype)
        other_ref[...] = total[...].T.astype(other_ref.dtype)


def back(err, weight, weight_other):
    layers, feat_shard, width = weight.shape
    rows = err.shape[1]
    small = pl.BlockSpec((rows, feat_shard), lambda m: (0, 0))
    large = pl.BlockSpec((1, feat_shard, width), lambda m: (m, 0, 0))
    half = jax.ShapeDtypeStruct((rows, feat_shard), jnp.bfloat16)
    return pl.pallas_call(
        back_kernel,
        out_shape=[jax.ShapeDtypeStruct((rows, feat_shard), jnp.float32), half, half],
        grid=(layers,),
        in_specs=[pl.BlockSpec((1, rows, width), lambda m: (m, 0, 0)), large, large],
        out_specs=[small, small, small],
        scratch_shapes=[pltpu.VMEM((feat_shard, rows), jnp.float32)] * 2,
        compiler_params=PARAMS,
        cost_estimate=cost(4 * rows * weight.size, weight, weight_other, err),
    )(err, weight, weight_other)


def grad_kernel(codes_ref, mine_ref, theirs_ref, out_ref):
    err = jnp.concatenate([mine_ref[0], theirs_ref[0]], axis=0)
    total = product(codes_ref[...], err, 1, 0)
    out_ref[0] = total.astype(out_ref.dtype)


def decoder_grad(codes, mine, theirs):
    layers, half, width = mine.shape
    feat_shard = codes.shape[0]
    err = pl.BlockSpec((1, half, width), lambda m: (m, 0, 0))
    out = jax.ShapeDtypeStruct((layers, feat_shard, width), jnp.bfloat16)
    return pl.pallas_call(
        grad_kernel,
        out_shape=out,
        grid=(layers,),
        in_specs=[pl.BlockSpec(codes.shape, lambda m: (0, 0)), err, err],
        out_specs=pl.BlockSpec((1, feat_shard, width), lambda m: (m, 0, 0)),
        compiler_params=PARAMS,
        cost_estimate=cost(4 * feat_shard * mine.size, mine, theirs, out),
    )(codes, mine, theirs)


def sum_kernel(parts_ref, out_ref):
    total = parts_ref[0].astype(jnp.float32)
    for part in range(1, parts_ref.shape[0]):
        total = total + parts_ref[part].astype(jnp.float32)
    out_ref[...] = total.astype(out_ref.dtype)


def sum_parts(parts, pieces=2):
    count, rows, width = parts.shape
    out = jax.ShapeDtypeStruct((rows, width), jnp.bfloat16)
    return pl.pallas_call(
        sum_kernel,
        out_shape=out,
        grid=(pieces,),
        in_specs=[pl.BlockSpec((count, rows // pieces, width), lambda i: (0, i, 0))],
        out_specs=pl.BlockSpec((rows // pieces, width), lambda i: (i, 0)),
        compiler_params=PARAMS,
        cost_estimate=cost(parts.size, parts, out),
    )(parts)


def ordered(first, mine, other, axis):
    return jnp.where(
        first, jnp.concatenate([mine, other], axis), jnp.concatenate([other, mine], axis)
    )


def body(resid, enc_weight, enc_bias, active, dec_weight, target):
    layers, feat_shard, width = dec_weight.shape[1:]
    layer = lax.axis_index("y")
    core0 = lax.axis_index("core") == 0
    tok0 = lax.axis_index("tok") == 0
    zs, peers = lax.axis_size("zh"), 2 * lax.axis_size("zh")
    resid_local = resid[0]
    weight = dec_weight[0]
    weight_kept = pltpu.with_memory_space_constraint(weight, pltpu.HBM)
    weight_other = lax.ppermute(weight, "core", SWAP)
    preact = (
        jnp.dot(resid_local, enc_weight[0], preferred_element_type=jnp.float32)
        + enc_bias[0][None, :]
    )
    codes_local = jnp.where(active[0] == 1, preact, 0.0).astype(jnp.bfloat16)
    tokens = 2 * codes_local.shape[0]
    half, quarter = tokens // 2, tokens // 4
    inv_root = 1.0 / math.sqrt(tokens)

    split = codes_local.reshape(zs // 2, 2, 2, 2, ROWS, feat_shard).transpose(3, 1, 0, 2, 4, 5)
    local_mine = jnp.where(core0, split[0], split[1])
    local_theirs = jnp.where(core0, split[1], split[0])
    from_tok = lax.ppermute(jnp.stack([local_mine, local_theirs]), "tok", SWAP)
    from_core = lax.ppermute(local_theirs, "core", SWAP)
    from_cross = lax.ppermute(local_theirs, BOTH, CROSS)

    def whole(mine, other):
        return ordered(tok0, mine, other, 1).reshape(half, feat_shard)

    codes_mine = whole(local_mine, from_tok[0])
    codes_theirs = whole(local_theirs, from_tok[1])
    codes_other = whole(from_core, from_cross)

    rows = resid_local.shape[0] // 2
    mask_late = (active[0] == 1).astype(jnp.bfloat16)
    fetch = jnp.where(core0, resid_local[:rows], resid_local[rows:])
    codes_mine, fetch, mask_late = lax.optimization_barrier((codes_mine, fetch, mask_late))
    fetched = lax.ppermute(fetch, "tok", SWAP)
    mask_other = lax.ppermute(mask_late, "tok", SWAP)
    pair = decode(layer, codes_mine, codes_other, weight_kept, weight_other)
    by_source = lax.all_to_all(
        pair.reshape(2 * layers, quarter, width), ("y", "zl"), 0, 0
    )
    by_source, fetched, mask_other = lax.optimization_barrier((by_source, fetched, mask_other))
    fetched_other = lax.ppermute(fetched, "core", SWAP)
    summed = sum_parts(by_source).reshape(peers, ROWS, width)
    by_group = lax.all_to_all(summed, ("zh", "xh"), 0, 0)
    by_group, fetched_other = lax.optimization_barrier((by_group, fetched_other))
    decoded = jnp.sum(by_group.astype(jnp.float32), axis=0)
    error = ((decoded - target[0].astype(jnp.float32)) * inv_root).astype(jnp.bfloat16)

    own = lax.all_to_all(
        jnp.broadcast_to(error[None], (peers, ROWS, width)), ("zh", "xh"), 0, 0
    )
    own, fetched, fetched_other, mask_late, mask_other, codes_mine, codes_theirs, decoded = (
        lax.optimization_barrier(
            (own, fetched, fetched_other, mask_late, mask_other, codes_mine, codes_theirs, decoded)
        )
    )
    own = own.reshape(quarter, width)
    wanted = (jnp.arange(2 * layers) // 2 <= layer)[:, None, None]
    spread = jnp.where(wanted, own[None], jnp.zeros((), own.dtype))
    err_mine = lax.all_to_all(spread, ("y", "zl"), 0, 0).reshape(layers, half, width)
    resid_other = ordered(core0, fetched, fetched_other, 0)
    resid_all = ordered(tok0, resid_local, resid_other, 0)
    mask = ordered(tok0, mask_late, mask_other, 0)
    codes_all = jnp.concatenate([codes_mine, codes_theirs], axis=0).T
    recon = decoded.astype(jnp.bfloat16)[None]
    err_mine, resid_all, mask, codes_all, recon = lax.optimization_barrier(
        (err_mine, resid_all, mask, codes_all, recon)
    )
    err_theirs = lax.ppermute(err_mine, "core", SWAP)

    feat_mine, feat_sent, feat_other = back(err_mine, weight_kept, weight_other)
    got_tok = lax.ppermute(feat_sent, "tok", SWAP)
    got_cross = lax.ppermute(feat_other, BOTH, CROSS)
    got_core = lax.ppermute(feat_other, "core", SWAP)

    dec_grad = decoder_grad(codes_all, err_mine, err_theirs)
    got_tok, got_core, got_cross, dec_grad = lax.optimization_barrier(
        (got_tok, got_core, got_cross, dec_grad)
    )
    grad_mine = feat_mine + got_tok.astype(jnp.float32)
    grad_theirs = got_core.astype(jnp.float32) + got_cross.astype(jnp.float32)
    feat_grad = ordered(core0, grad_mine[None], grad_theirs[None], 0)
    feat_grad = feat_grad.reshape(2, 2, zs, 2, ROWS, feat_shard).transpose(2, 1, 3, 0, 4, 5)
    feat_grad = feat_grad.reshape(tokens, feat_shard)
    masked = jnp.where(mask > 0, feat_grad, 0.0)
    bias_grad = jnp.sum(masked, axis=0)
    enc_grad = lax.dot_general(
        resid_all,
        masked.astype(jnp.bfloat16),
        (((0,), (0,)), ((), ())),
        preferred_element_type=jnp.float32,
    ).astype(jnp.bfloat16)
    return recon, enc_grad[None], bias_grad[None], dec_grad[None]


def solution(mesh):
    layer, feat, tok = (mesh.shape[name] for name in ("layer", "feat", "tok"))
    fine = Mesh(
        mesh.devices.reshape(layer, feat // 8, 2, 2, 2, tok),
        ("y", "zh", "zl", "xh", "core", "tok"),
    )
    feat_axes = ("zh", "zl", "xh", "core")
    in_specs = (
        P("y", "tok", None),
        P("y", None, feat_axes),
        P("y", feat_axes),
        P("y", "tok", feat_axes),
        P("y", None, feat_axes, "tok"),
        P("y", feat_axes, "tok"),
    )
    out_specs = (
        P("y", feat_axes, "tok"),
        P("y", None, feat_axes),
        P("y", feat_axes),
        P("y", None, feat_axes, "tok"),
    )
    return jax.shard_map(body, mesh=fine, in_specs=in_specs, out_specs=out_specs, check_vma=False)
```

```python
import math

import jax
import jax.numpy as jnp
from jax import lax
from jax.experimental import pallas as pl
from jax.experimental.pallas import tpu as pltpu
from jax.sharding import Mesh, PartitionSpec as P

SWAP = [(0, 1), (1, 0)]
CROSS = [(0, 3), (1, 2), (2, 1), (3, 0)]
BOTH = ("core", "tok")
ROWS = 8


PARAMS = pltpu.CompilerParams(vmem_limit_bytes=12 * 1024 * 1024)


def cost(flops, *arrays):
    moved = sum(a.size * a.dtype.itemsize for a in arrays)
    return pl.CostEstimate(flops=flops, bytes_accessed=moved, transcendentals=0)


def product(left, right, left_dim, right_dim):
    dims = (((left_dim,), (right_dim,)), ((), ()))
    return lax.dot_general(left, right, dims, preferred_element_type=jnp.float32)


def decode_kernel(layer_ref, mine_ref, other_ref, weight_ref, weight_other_ref, out_ref):
    used = pl.program_id(0) >= layer_ref[0]

    @pl.when(used)
    def _():
        total = product(mine_ref[...], weight_ref[0], 1, 0)
        total = total + product(other_ref[...], weight_other_ref[0], 1, 0)
        out_ref[0] = total.astype(out_ref.dtype)

    @pl.when(jnp.logical_not(used))
    def _():
        out_ref[...] = jnp.zeros_like(out_ref)


def decode(layer, mine, other, weight, weight_other):
    layers, feat_shard, width = weight.shape
    rows = mine.shape[0]
    small = pl.BlockSpec((rows, feat_shard), lambda m, _: (0, 0))
    large = pl.BlockSpec((1, feat_shard, width), lambda m, _: (m, 0, 0))
    out = jax.ShapeDtypeStruct((layers, rows, width), jnp.bfloat16)
    return pl.pallas_call(
        decode_kernel,
        out_shape=pltpu.HBM(out.shape, out.dtype),
        grid_spec=pltpu.PrefetchScalarGridSpec(
            num_scalar_prefetch=1,
            grid=(layers,),
            in_specs=[small, small, large, large],
            out_specs=pl.BlockSpec((1, rows, width), lambda m, _: (m, 0, 0)),
        ),
        compiler_params=PARAMS,
        cost_estimate=cost(4 * rows * weight.size, weight, weight_other, out),
    )(layer.reshape(1), mine, other, weight, weight_other)


def back_kernel(err_ref, weight_ref, weight_other_ref, mine_ref, sent_ref, other_ref):
    mine = other = 0.0
    for target in range(err_ref.shape[0]):
        err = err_ref[target].T
        mine = mine + product(weight_ref[target], err, 1, 0)
        other = other + product(weight_other_ref[target], err, 1, 0)
    mine = mine.T
    mine_ref[...] = mine
    sent_ref[...] = mine.astype(sent_ref.dtype)
    other_ref[...] = other.T.astype(other_ref.dtype)


def back(err, weight, weight_other):
    shape = (err.shape[1], weight.shape[1])
    half = jax.ShapeDtypeStruct(shape, jnp.bfloat16)
    held = pl.BlockSpec(memory_space=pltpu.VMEM)
    return pl.pallas_call(
        back_kernel,
        out_shape=[jax.ShapeDtypeStruct(shape, jnp.float32), half, half],
        in_specs=[held] * 3,
        out_specs=[held] * 3,
        compiler_params=pltpu.CompilerParams(vmem_limit_bytes=20 * 1024 * 1024),
        cost_estimate=cost(4 * shape[0] * weight.size, weight, weight_other, err),
    )(err, weight, weight_other)


def grad_kernel(codes_ref, mine_ref, theirs_ref, out_ref):
    err = jnp.concatenate([mine_ref[0], theirs_ref[0]], axis=0)
    total = product(codes_ref[...], err, 1, 0)
    out_ref[0] = total.astype(out_ref.dtype)


def decoder_grad(codes, mine, theirs):
    layers, half, width = mine.shape
    feat_shard = codes.shape[0]
    err = pl.BlockSpec((1, half, width), lambda m: (m, 0, 0))
    out = jax.ShapeDtypeStruct((layers, feat_shard, width), jnp.bfloat16)
    return pl.pallas_call(
        grad_kernel,
        out_shape=out,
        grid=(layers,),
        in_specs=[pl.BlockSpec(codes.shape, lambda m: (0, 0)), err, err],
        out_specs=pl.BlockSpec((1, feat_shard, width), lambda m: (m, 0, 0)),
        compiler_params=PARAMS,
        cost_estimate=cost(4 * feat_shard * mine.size, mine, theirs, out),
    )(codes, mine, theirs)


def sum_kernel(parts_ref, out_ref):
    total = parts_ref[0].astype(jnp.float32)
    for part in range(1, parts_ref.shape[0]):
        total = total + parts_ref[part].astype(jnp.float32)
    out_ref[...] = total.astype(out_ref.dtype)


def sum_parts(parts, pieces=2):
    count, rows, width = parts.shape
    out = jax.ShapeDtypeStruct((rows, width), jnp.bfloat16)
    return pl.pallas_call(
        sum_kernel,
        out_shape=out,
        grid=(pieces,),
        in_specs=[pl.BlockSpec((count, rows // pieces, width), lambda i: (0, i, 0))],
        out_specs=pl.BlockSpec((rows // pieces, width), lambda i: (i, 0)),
        compiler_params=PARAMS,
        cost_estimate=cost(parts.size, parts, out),
    )(parts)


def ordered(first, mine, other, axis):
    return jnp.where(
        first, jnp.concatenate([mine, other], axis), jnp.concatenate([other, mine], axis)
    )


def body(resid, enc_weight, enc_bias, active, dec_weight, target):
    layers, feat_shard, width = dec_weight.shape[1:]
    layer = lax.axis_index("y")
    core0 = lax.axis_index("core") == 0
    tok0 = lax.axis_index("tok") == 0
    zs, peers = lax.axis_size("zh"), 2 * lax.axis_size("zh")
    resid_local = resid[0]
    weight = dec_weight[0]
    weight_kept = pltpu.with_memory_space_constraint(weight, pltpu.HBM)
    weight_other = lax.ppermute(weight, "core", SWAP)
    preact = (
        jnp.dot(resid_local, enc_weight[0], preferred_element_type=jnp.float32)
        + enc_bias[0][None, :]
    )
    codes_local = jnp.where(active[0] == 1, preact, 0.0).astype(jnp.bfloat16)
    tokens = 2 * codes_local.shape[0]
    half, quarter = tokens // 2, tokens // 4
    inv_root = 1.0 / math.sqrt(tokens)

    split = codes_local.reshape(zs // 2, 2, 2, 2, ROWS, feat_shard).transpose(3, 1, 0, 2, 4, 5)
    local_mine = jnp.where(core0, split[0], split[1])
    local_theirs = jnp.where(core0, split[1], split[0])
    from_tok = lax.ppermute(jnp.stack([local_mine, local_theirs]), "tok", SWAP)
    from_core = lax.ppermute(local_theirs, "core", SWAP)
    from_cross = lax.ppermute(local_theirs, BOTH, CROSS)

    def whole(mine, other):
        return ordered(tok0, mine, other, 1).reshape(half, feat_shard)

    codes_mine = whole(local_mine, from_tok[0])
    codes_theirs = whole(local_theirs, from_tok[1])
    codes_other = whole(from_core, from_cross)

    rows = resid_local.shape[0] // 2
    mask_late = (active[0] == 1).astype(jnp.bfloat16)
    fetch = jnp.where(core0, resid_local[:rows], resid_local[rows:])
    codes_mine, fetch, mask_late = lax.optimization_barrier((codes_mine, fetch, mask_late))
    fetched = lax.ppermute(fetch, "tok", SWAP)
    mask_other = lax.ppermute(mask_late, "tok", SWAP)
    pair = decode(layer, codes_mine, codes_other, weight_kept, weight_other)
    by_source = lax.all_to_all(
        pair.reshape(2 * layers, quarter, width), ("y", "zl"), 0, 0
    )
    by_source, fetched, mask_other = lax.optimization_barrier((by_source, fetched, mask_other))
    summed = sum_parts(by_source).reshape(peers, ROWS, width)
    by_group = lax.all_to_all(summed, ("zh", "xh"), 0, 0)
    decoded = jnp.sum(by_group.astype(jnp.float32), axis=0)
    error = ((decoded - target[0].astype(jnp.float32)) * inv_root).astype(jnp.bfloat16)

    own = lax.all_to_all(
        jnp.broadcast_to(error[None], (peers, ROWS, width)), ("zh", "xh"), 0, 0
    )
    own, fetched, mask_late, mask_other, codes_mine, codes_theirs, decoded, weight_late = (
        lax.optimization_barrier(
            (own, fetched, mask_late, mask_other, codes_mine, codes_theirs, decoded, weight)
        )
    )
    fetched_other = lax.ppermute(fetched, "core", SWAP)
    weight_late = jnp.where(layer >= 0, weight_late, jnp.zeros((), weight.dtype))
    own = own.reshape(quarter, width)
    wanted = (jnp.arange(2 * layers) // 2 <= layer)[:, None, None]
    spread = jnp.where(wanted, own[None], jnp.zeros((), own.dtype))
    err_mine = lax.all_to_all(spread, ("y", "zl"), 0, 0).reshape(layers, half, width)
    resid_other = ordered(core0, fetched, fetched_other, 0)
    resid_all = ordered(tok0, resid_local, resid_other, 0)
    mask = ordered(tok0, mask_late, mask_other, 0)
    codes_all = jnp.concatenate([codes_mine, codes_theirs], axis=0).T
    recon = decoded.astype(jnp.bfloat16)[None]
    err_mine, resid_all, mask, codes_all, recon, weight_late = lax.optimization_barrier(
        (err_mine, resid_all, mask, codes_all, recon, weight_late)
    )
    err_theirs = lax.ppermute(err_mine, "core", SWAP)

    feat_mine, feat_sent, feat_other = back(err_mine, weight_late, weight_other)
    got_tok = lax.ppermute(feat_sent, "tok", SWAP)
    got_cross = lax.ppermute(feat_other, BOTH, CROSS)
    got_core = lax.ppermute(feat_other, "core", SWAP)

    dec_grad = decoder_grad(codes_all, err_mine, err_theirs)
    got_tok, got_core, got_cross, dec_grad = lax.optimization_barrier(
        (got_tok, got_core, got_cross, dec_grad)
    )
    grad_mine = feat_mine + got_tok.astype(jnp.float32)
    grad_theirs = got_core.astype(jnp.float32) + got_cross.astype(jnp.float32)
    feat_grad = ordered(core0, grad_mine[None], grad_theirs[None], 0)
    feat_grad = feat_grad.reshape(2, 2, zs, 2, ROWS, feat_shard).transpose(2, 1, 3, 0, 4, 5)
    feat_grad = feat_grad.reshape(tokens, feat_shard)
    masked = jnp.where(mask > 0, feat_grad, 0.0)
    bias_grad = jnp.sum(masked, axis=0)
    enc_grad = lax.dot_general(
        resid_all,
        masked.astype(jnp.bfloat16),
        (((0,), (0,)), ((), ())),
        preferred_element_type=jnp.float32,
    ).astype(jnp.bfloat16)
    return recon, enc_grad[None], bias_grad[None], dec_grad[None]


def solution(mesh):
    layer, feat, tok = (mesh.shape[name] for name in ("layer", "feat", "tok"))
    fine = Mesh(
        mesh.devices.reshape(layer, feat // 8, 2, 2, 2, tok),
        ("y", "zh", "zl", "xh", "core", "tok"),
    )
    feat_axes = ("zh", "zl", "xh", "core")
    in_specs = (
        P("y", "tok", None),
        P("y", None, feat_axes),
        P("y", feat_axes),
        P("y", "tok", feat_axes),
        P("y", None, feat_axes, "tok"),
        P("y", feat_axes, "tok"),
    )
    out_specs = (
        P("y", feat_axes, "tok"),
        P("y", None, feat_axes),
        P("y", feat_axes),
        P("y", None, feat_axes, "tok"),
    )
    return jax.shard_map(body, mesh=fine, in_specs=in_specs, out_specs=out_specs, check_vma=False)
```

```python
import math

import jax
import jax.numpy as jnp
from jax import lax
from jax.experimental import pallas as pl
from jax.experimental.pallas import tpu as pltpu
from jax.sharding import Mesh, PartitionSpec as P

SWAP = [(0, 1), (1, 0)]
CROSS = [(0, 3), (1, 2), (2, 1), (3, 0)]
BOTH = ("core", "tok")
ROWS = 8


PARAMS = pltpu.CompilerParams(vmem_limit_bytes=12 * 1024 * 1024)


def cost(flops, *arrays):
    moved = sum(a.size * a.dtype.itemsize for a in arrays)
    return pl.CostEstimate(flops=flops, bytes_accessed=moved, transcendentals=0)


def product(left, right, left_dim, right_dim):
    dims = (((left_dim,), (right_dim,)), ((), ()))
    return lax.dot_general(left, right, dims, preferred_element_type=jnp.float32)


def decode_kernel(layer_ref, mine_ref, other_ref, weight_ref, weight_other_ref, out_ref):
    used = pl.program_id(0) >= layer_ref[0]

    @pl.when(used)
    def _():
        total = product(mine_ref[...], weight_ref[0], 1, 0)
        total = total + product(other_ref[...], weight_other_ref[0], 1, 0)
        out_ref[0] = total.astype(out_ref.dtype)

    @pl.when(jnp.logical_not(used))
    def _():
        out_ref[...] = jnp.zeros_like(out_ref)


def decode(layer, mine, other, weight, weight_other):
    layers, feat_shard, width = weight.shape
    rows = mine.shape[0]
    small = pl.BlockSpec((rows, feat_shard), lambda m, _: (0, 0))
    large = pl.BlockSpec((1, feat_shard, width), lambda m, _: (m, 0, 0))
    out = jax.ShapeDtypeStruct((layers, rows, width), jnp.bfloat16)
    return pl.pallas_call(
        decode_kernel,
        out_shape=pltpu.HBM(out.shape, out.dtype),
        grid_spec=pltpu.PrefetchScalarGridSpec(
            num_scalar_prefetch=1,
            grid=(layers,),
            in_specs=[small, small, large, large],
            out_specs=pl.BlockSpec((1, rows, width), lambda m, _: (m, 0, 0)),
        ),
        compiler_params=PARAMS,
        cost_estimate=cost(4 * rows * weight.size, weight, weight_other, out),
    )(layer.reshape(1), mine, other, weight, weight_other)


def back_kernel(
    err_ref, weight_ref, weight_other_ref, mine_ref, sent_ref, other_ref, total_mine, total
):
    step = pl.program_id(0)
    err = err_ref[0].T
    mine = product(weight_ref[0], err, 1, 0)
    other = product(weight_other_ref[0], err, 1, 0)

    @pl.when(step == 0)
    def _():
        total_mine[...] = mine
        total[...] = other

    @pl.when(step > 0)
    def _():
        total_mine[...] += mine
        total[...] += other

    @pl.when(step == pl.num_programs(0) - 1)
    def _():
        whole = total_mine[...].T
        mine_ref[...] = whole
        sent_ref[...] = whole.astype(sent_ref.dtype)
        other_ref[...] = total[...].T.astype(other_ref.dtype)


def back(err, weight, weight_other):
    layers, feat_shard, width = weight.shape
    rows = err.shape[1]
    small = pl.BlockSpec((rows, feat_shard), lambda m: (0, 0))
    large = pl.BlockSpec((1, feat_shard, width), lambda m: (m, 0, 0))
    half = jax.ShapeDtypeStruct((rows, feat_shard), jnp.bfloat16)
    return pl.pallas_call(
        back_kernel,
        out_shape=[jax.ShapeDtypeStruct((rows, feat_shard), jnp.float32), half, half],
        grid=(layers,),
        in_specs=[pl.BlockSpec((1, rows, width), lambda m: (m, 0, 0)), large, large],
        out_specs=[small, small, small],
        scratch_shapes=[pltpu.VMEM((feat_shard, rows), jnp.float32)] * 2,
        compiler_params=PARAMS,
        cost_estimate=cost(4 * rows * weight.size, weight, weight_other, err),
    )(err, weight, weight_other)


def grad_kernel(codes_ref, mine_ref, theirs_ref, out_ref):
    err = jnp.concatenate([mine_ref[0], theirs_ref[0]], axis=0)
    total = product(codes_ref[...], err, 1, 0)
    out_ref[0] = total.astype(out_ref.dtype)


def decoder_grad(codes, mine, theirs):
    layers, half, width = mine.shape
    feat_shard = codes.shape[0]
    err = pl.BlockSpec((1, half, width), lambda m: (m, 0, 0))
    out = jax.ShapeDtypeStruct((layers, feat_shard, width), jnp.bfloat16)
    return pl.pallas_call(
        grad_kernel,
        out_shape=out,
        grid=(layers,),
        in_specs=[pl.BlockSpec(codes.shape, lambda m: (0, 0)), err, err],
        out_specs=pl.BlockSpec((1, feat_shard, width), lambda m: (m, 0, 0)),
        compiler_params=PARAMS,
        cost_estimate=cost(4 * feat_shard * mine.size, mine, theirs, out),
    )(codes, mine, theirs)


def sum_kernel(parts_ref, out_ref):
    total = parts_ref[0].astype(jnp.float32)
    for part in range(1, parts_ref.shape[0]):
        total = total + parts_ref[part].astype(jnp.float32)
    out_ref[...] = total.astype(out_ref.dtype)


def sum_parts(parts, pieces=2):
    count, rows, width = parts.shape
    out = jax.ShapeDtypeStruct((rows, width), jnp.bfloat16)
    return pl.pallas_call(
        sum_kernel,
        out_shape=out,
        grid=(pieces,),
        in_specs=[pl.BlockSpec((count, rows // pieces, width), lambda i: (0, i, 0))],
        out_specs=pl.BlockSpec((rows // pieces, width), lambda i: (i, 0)),
        compiler_params=PARAMS,
        cost_estimate=cost(parts.size, parts, out),
    )(parts)


def ordered(first, mine, other, axis):
    return jnp.where(
        first, jnp.concatenate([mine, other], axis), jnp.concatenate([other, mine], axis)
    )


def body(resid, enc_weight, enc_bias, active, dec_weight, target):
    layers, feat_shard, width = dec_weight.shape[1:]
    layer = lax.axis_index("y")
    core0 = lax.axis_index("core") == 0
    tok0 = lax.axis_index("tok") == 0
    zs, peers = lax.axis_size("zh"), 2 * lax.axis_size("zh")
    resid_local = resid[0]
    weight = dec_weight[0]
    weight_kept = pltpu.with_memory_space_constraint(weight, pltpu.HBM)
    weight_other = lax.ppermute(weight, "core", SWAP)
    preact = (
        jnp.dot(resid_local, enc_weight[0], preferred_element_type=jnp.float32)
        + enc_bias[0][None, :]
    )
    codes_local = jnp.where(active[0] == 1, preact, 0.0).astype(jnp.bfloat16)
    tokens = 2 * codes_local.shape[0]
    half, quarter = tokens // 2, tokens // 4
    inv_root = 1.0 / math.sqrt(tokens)

    split = codes_local.reshape(zs // 2, 2, 2, 2, ROWS, feat_shard).transpose(3, 1, 0, 2, 4, 5)
    local_mine = jnp.where(core0, split[0], split[1])
    local_theirs = jnp.where(core0, split[1], split[0])
    from_tok = lax.ppermute(jnp.stack([local_mine, local_theirs]), "tok", SWAP)
    from_core = lax.ppermute(local_theirs, "core", SWAP)
    from_cross = lax.ppermute(local_theirs, BOTH, CROSS)

    def whole(mine, other):
        return ordered(tok0, mine, other, 1).reshape(half, feat_shard)

    codes_mine = whole(local_mine, from_tok[0])
    codes_theirs = whole(local_theirs, from_tok[1])
    codes_other = whole(from_core, from_cross)

    rows = resid_local.shape[0] // 2
    mask_late = (active[0] == 1).astype(jnp.bfloat16)
    fetch = jnp.where(core0, resid_local[:rows], resid_local[rows:])
    codes_mine, fetch, mask_late = lax.optimization_barrier((codes_mine, fetch, mask_late))
    fetched = lax.ppermute(fetch, "tok", SWAP)
    mask_other = lax.ppermute(mask_late, "tok", SWAP)
    pair = decode(layer, codes_mine, codes_other, weight_kept, weight_other)
    by_source = lax.all_to_all(
        pair.reshape(2 * layers, quarter, width), ("y", "zl"), 0, 0
    )
    by_source, fetched, mask_other = lax.optimization_barrier((by_source, fetched, mask_other))
    summed = sum_parts(by_source).reshape(peers, ROWS, width)
    by_group = lax.all_to_all(summed, ("zh", "xh"), 0, 0)
    decoded = jnp.sum(by_group.astype(jnp.float32), axis=0)
    error = ((decoded - target[0].astype(jnp.float32)) * inv_root).astype(jnp.bfloat16)

    own = lax.all_to_all(
        jnp.broadcast_to(error[None], (peers, ROWS, width)), ("zh", "xh"), 0, 0
    )
    own, fetched, mask_late, mask_other, codes_mine, codes_theirs, decoded = (
        lax.optimization_barrier(
            (own, fetched, mask_late, mask_other, codes_mine, codes_theirs, decoded)
        )
    )
    fetched_other = lax.ppermute(fetched, "core", SWAP)
    own = own.reshape(quarter, width)
    wanted = (jnp.arange(2 * layers) // 2 <= layer)[:, None, None]
    spread = jnp.where(wanted, own[None], jnp.zeros((), own.dtype))
    err_mine = lax.all_to_all(spread, ("y", "zl"), 0, 0).reshape(layers, half, width)
    resid_other = ordered(core0, fetched, fetched_other, 0)
    resid_all = ordered(tok0, resid_local, resid_other, 0)
    mask = ordered(tok0, mask_late, mask_other, 0)
    codes_all = jnp.concatenate([codes_mine, codes_theirs], axis=0).T
    recon = decoded.astype(jnp.bfloat16)[None]
    err_mine, resid_all, mask, codes_all, recon = lax.optimization_barrier(
        (err_mine, resid_all, mask, codes_all, recon)
    )
    err_theirs = lax.ppermute(err_mine, "core", SWAP)

    feat_mine, feat_sent, feat_other = back(err_mine, weight_kept, weight_other)
    got_tok = lax.ppermute(feat_sent, "tok", SWAP)
    got_cross = lax.ppermute(feat_other, BOTH, CROSS)
    got_core = lax.ppermute(feat_other, "core", SWAP)

    dec_grad = decoder_grad(codes_all, err_mine, err_theirs)
    got_tok, got_core, got_cross, dec_grad = lax.optimization_barrier(
        (got_tok, got_core, got_cross, dec_grad)
    )
    grad_mine = feat_mine + got_tok.astype(jnp.float32)
    grad_theirs = got_core.astype(jnp.float32) + got_cross.astype(jnp.float32)
    feat_grad = ordered(core0, grad_mine[None], grad_theirs[None], 0)
    feat_grad = feat_grad.reshape(2, 2, zs, 2, ROWS, feat_shard).transpose(2, 1, 3, 0, 4, 5)
    feat_grad = feat_grad.reshape(tokens, feat_shard)
    masked = jnp.where(mask > 0, feat_grad, 0.0)
    bias_grad = jnp.sum(masked, axis=0)
    enc_grad = lax.dot_general(
        resid_all,
        masked.astype(jnp.bfloat16),
        (((0,), (0,)), ((), ())),
        preferred_element_type=jnp.float32,
    ).astype(jnp.bfloat16)
    return recon, enc_grad[None], bias_grad[None], dec_grad[None]


def solution(mesh):
    layer, feat, tok = (mesh.shape[name] for name in ("layer", "feat", "tok"))
    fine = Mesh(
        mesh.devices.reshape(layer, feat // 8, 2, 2, 2, tok),
        ("y", "zh", "zl", "xh", "core", "tok"),
    )
    feat_axes = ("zh", "zl", "xh", "core")
    in_specs = (
        P("y", "tok", None),
        P("y", None, feat_axes),
        P("y", feat_axes),
        P("y", "tok", feat_axes),
        P("y", None, feat_axes, "tok"),
        P("y", feat_axes, "tok"),
    )
    out_specs = (
        P("y", feat_axes, "tok"),
        P("y", None, feat_axes),
        P("y", feat_axes),
        P("y", None, feat_axes, "tok"),
    )
    return jax.shard_map(body, mesh=fine, in_specs=in_specs, out_specs=out_specs, check_vma=False)
```
